512 devices in a mesh: pipe: 16 (over y, x_hi, core), ctx: 32 (over z, x_lo).
Axes of the slice: x: 4 (x_hi: 2, x_lo: 2; x = x_hi * 2 + x_lo), y: 4, z: 16, core: 2. Of those that a mesh axis runs over, the one named last changes fastest.
Arguments:
- x_in: bfloat16 [16, 1, 5120, 2048], P('pipe', None, 'ctx'), may hold values from -6 to 6
- q_gain: float32 [16, 2048], P('pipe'), may hold values from 0.1 to 1.9
- key_gain_per_layer: float32 [16, 2048], P('pipe'), may hold values from 0.1 to 1.9
- out_gain: float32 [16, 2048], P('pipe'), may hold values from 0.1 to 1.9
- log_decay: float32 [16, 5120, 16], P('pipe', 'ctx'), may hold values from -4 to 0, as said below
- out_weight: bfloat16 [16, 2048, 2048], P('pipe', 'ctx'), may hold values from -0.125 to 0.125
Outputs:
- out: bfloat16 [16, 1, 5120, 2048], P('pipe', None, 'ctx')
The draws below stay inside these ranges and needn't reach their ends.
Inputs may be any that keep to these rules, and one draw needn't show every extreme that they name: `log_decay`: every entry is negative.
All inputs are finite; a program needn't handle non-finite values.
Results may differ from the reference program's by a relative error of at most 0.014.
Values may be sent and summed in bfloat16 or wider, within the bound.
A program may use at most 128 MiB of HBM per device.

```python
import math
import jax
import jax.numpy as jnp
from jax import lax

HEADS = 16
WIDTH = 2048
MICRO = 1
TOK_DEV = 160
TOKENS = 5120
SECTIONS = 16


def draw_log_decay(key, part):
    keys = jax.random.split(key, 7)
    share = 0.5
    quick = jax.random.uniform(keys[0], (SECTIONS, 1, HEADS)) < share
    slow_rate = jax.random.uniform(keys[1], (SECTIONS, 1, HEADS), minval=0.1, maxval=0.4) / TOKENS
    quick_rate = jax.random.uniform(keys[2], (SECTIONS, 1, HEADS), minval=2.5, maxval=4.5) / TOK_DEV
    rate = jnp.where(quick, quick_rate, slow_rate)
    blocks = TOKENS // TOK_DEV
    block_factor = jnp.exp(jax.random.uniform(keys[3], (SECTIONS, blocks, 1, HEADS), minval=-0.69, maxval=0.69))
    block_factor = jnp.broadcast_to(block_factor, (SECTIONS, blocks, TOK_DEV, HEADS)).reshape(SECTIONS, TOKENS, HEADS)
    place_factor = jnp.exp(jax.random.uniform(keys[4], (SECTIONS, TOKENS, HEADS), minval=-0.69, maxval=0.69))
    starting_shift = -rate * block_factor * place_factor
    spots = jax.random.randint(keys[5], (SECTIONS, 2), 0, TOKENS)
    retain_multiplier = jax.random.uniform(keys[6], (SECTIONS, 2), minval=0.5, maxval=0.8)
    match_tally = jnp.arange(TOKENS)[None, :, None] == spots[:, None, :]
    span_size = jnp.sum(jnp.where(match_tally, jnp.log(retain_multiplier)[:, None, :], 0.0), axis=2)
    return (starting_shift + span_size[:, :, None]).astype(jnp.float32)


def level_of(stream_key, dims, cuts, smallest, high):
    gain, own = 1.0, jax.random.fold_in(stream_key, 6)
    for dim, shards_of in cuts:
        steps = jnp.exp(jax.random.uniform(jax.random.fold_in(own, dim), (shards_of,), jnp.float32, smallest / len(cuts), high / len(cuts)))
        gain = gain * jnp.repeat(steps, dims[dim] // shards_of).reshape([-1 if axis == dim else 1 for axis in range(len(dims))])
    return gain


def scatter_about(stream_key, dims, scale, bound, cuts=(), dtype=jnp.bfloat16):
    result = scale * jax.random.normal(stream_key, dims, jnp.float32)
    if cuts:
        result = result * level_of(stream_key, dims, cuts, -0.22, 0.18)
    return jnp.clip(result, -bound, bound).astype(dtype)


def setup_inputs(seed: int = 0) -> dict:
    seeds = jax.random.split(jax.random.key(seed), 7)
    return {
        "x_in": scatter_about(seeds[0], (SECTIONS, MICRO, TOKENS, WIDTH), 1.0, 6.0, ((0, 16), (2, 32))),
        "q_gain": jnp.clip(1.0 + 0.18 * jax.random.normal(seeds[1], (SECTIONS, WIDTH), jnp.float32), 0.1, 1.9),
        "key_gain_per_layer": jnp.clip(1.0 + 0.18 * jax.random.normal(seeds[2], (SECTIONS, WIDTH), jnp.float32), 0.1, 1.9),
        "out_gain": jnp.clip(1.0 + 0.18 * jax.random.normal(seeds[3], (SECTIONS, WIDTH), jnp.float32), 0.1, 1.9),
        "log_decay": draw_log_decay(jax.random.fold_in(seeds[6], 71), 0),
        "out_weight": scatter_about(seeds[5], (SECTIONS, WIDTH, WIDTH), WIDTH ** -0.5, 0.125, ((0, 16), (1, 32))),
    }


EPS_RMS = 1e-06
TINY_NORM_GUARD = 1e-05
HIGH = lax.Precision.HIGHEST

def rounded(array):
    return lax.optimization_barrier(array.astype(jnp.bfloat16))

def rotate(values, places):
    half = values.shape[-1] // 2
    freqs = jnp.exp(-math.log(10000.0) * (2.0 * jnp.arange(half).astype(jnp.float32) / values.shape[-1]))
    angles = places[:, None] * freqs[None, :]
    cosine = jnp.cos(angles)[None, :, None, :]
    sine = jnp.sin(angles)[None, :, None, :]
    bottom_portion = values[..., :half]
    upper_half = values[..., half:]
    return jnp.concatenate([bottom_portion * cosine - upper_half * sine, upper_half * cosine + bottom_portion * sine], axis=-1)

def layer(x, q_gain, key_gain_per_layer, out_gain, log_decay, out_weight):
    micro, length, width = x.shape
    heads = log_decay.shape[-1]
    size = width // heads
    floats = x.astype(jnp.float32)
    normed = floats * lax.rsqrt(lax.optimization_barrier(jnp.mean(floats * floats, axis=-1, keepdims=True)) + EPS_RMS)
    places = jnp.arange(length).astype(jnp.float32)
    query = rounded(rotate((normed * q_gain).reshape(micro, length, heads, size), places))
    key_rot = rounded(rotate((normed * key_gain_per_layer).reshape(micro, length, heads, size), places))
    value = rounded(normed.reshape(micro, length, heads, size))
    blocks = length // TOK_DEV

    def split(array):
        return jnp.swapaxes(array.reshape(micro, blocks, TOK_DEV, heads, size), 0, 1)
    decays = log_decay.reshape(blocks, TOK_DEV, heads)
    lower = jnp.arange(TOK_DEV)[:, None] >= jnp.arange(TOK_DEV)[None, :]

    def step_forward(state, block):
        q_block, key_block_rows, v_block, a_block = block
        q_f = q_block.astype(jnp.float32)
        k_f = key_block_rows.astype(jnp.float32)
        v_f = v_block.astype(jnp.float32)
        running = jnp.cumsum(a_block, axis=0)
        scores = jnp.einsum('mnhd,mkhd->mhnk', q_f, k_f, precision=HIGH)
        across = running.T
        dispersion_width = across[:, :, None] - across[:, None, :]
        weight = jnp.exp(jnp.where(lower[None], dispersion_width, -1e+30))
        probs = rounded(scores * weight[None]).astype(jnp.float32)
        inner = jnp.einsum('mhnk,mkhd->mnhd', probs, v_f, precision=HIGH)
        carried = jnp.einsum('mnhd,mhde->mnhe', q_f, state.astype(jnp.float32), precision=HIGH)
        carried = carried * jnp.exp(running)[None, :, :, None]
        final_run = running[-1]
        shrunk = rounded(k_f * jnp.exp(final_run[None, :] - running)[None, :, :, None]).astype(jnp.float32)
        local_shard_state = rounded(jnp.einsum('mkhd,mkhe->mhde', shrunk, v_f, precision=HIGH)).astype(jnp.float32)
        total = rounded(final_run).astype(jnp.float32)
        new_state = (local_shard_state + jnp.exp(total)[None, :, None, None] * state.astype(jnp.float32)).astype(jnp.bfloat16)
        return (new_state, inner + carried)
    start_state = jnp.zeros((micro, heads, size, size), jnp.bfloat16)
    _, mixed = lax.scan(step_forward, start_state, (split(query), split(key_rot), split(value), decays))
    mixed = jnp.swapaxes(mixed, 0, 1).reshape(micro, length, heads, size)
    centre = mixed - lax.optimization_barrier(jnp.mean(mixed, axis=-1, keepdims=True))
    normal = centre * lax.rsqrt(lax.optimization_barrier(jnp.mean(centre * centre, axis=-1, keepdims=True)) + TINY_NORM_GUARD)
    scaled = rounded(normal.reshape(micro, length, width) * out_gain)
    product = jnp.dot(scaled.reshape(micro * length, width), out_weight, preferred_element_type=jnp.float32)
    return (floats + product.reshape(micro, length, width)).astype(jnp.bfloat16)

def apply_section(packed):
    return layer(packed[0], packed[1], packed[2], packed[3], packed[4], packed[5])

def reference(x_in, q_gain, key_gain_per_layer, out_gain, log_decay, out_weight):
    first = lax.map(apply_section, (x_in, q_gain, key_gain_per_layer, out_gain, log_decay, out_weight))
    return jnp.roll(first, 1, axis=0)
```

```python
import jax
import jax.numpy as jnp
import numpy as np
from jax import lax
from jax.experimental import pallas as pl
from jax.experimental.pallas import tpu as pltpu
from jax.sharding import PartitionSpec as P

EPS_RMS = 1e-06
EPS_NORM = 1e-05
MESH = pl.DeviceIdType.MESH
BF, F32 = jnp.bfloat16, jnp.float32
ROWS, WIDTH, HALF, HEAD, HEADS, OWN = 160, 2048, 1024, 128, 16, 8
Z, SUBS, PARTS, COLS = 16, 4, 4, 256
SUB = 128 // SUBS


def tables():
    freqs = 10000.0 ** (-2.0 * np.arange(64) / 128.0)
    freqs = np.concatenate([freqs, freqs])[None, :]
    sign = np.where(np.arange(128) < 64, -1.0, 1.0)[None, :]
    coarse = np.arange(32)[:, None] * float(ROWS) * freqs
    fine = np.arange(ROWS)[:, None] * freqs
    return tuple(
        np.stack([np.cos(a), sign * np.sin(a), np.sin(a)]).astype(np.float32) for a in (coarse, fine)
    )


def remote(src, dst, send, recv, device):
    return pltpu.make_async_remote_copy(
        src_ref=src, dst_ref=dst, send_sem=send, recv_sem=recv, device_id=device, device_id_type=MESH
    )


def dot(a, b, dims=((1,), (0,)), precision=None):
    return lax.dot_general(a, b, (dims, ((), ())), precision=precision, preferred_element_type=F32)


def kernel(
    x_ref, qg_ref, kg_ref, og_ref, ld_ref, w_ref, coarse_ref, fine_ref,
    out_ref,
    xh, iv, ldh, rb, rt, cs, sn, kb, vb, qb, st, inner, zs, zr, eo, ei, wz, act, ost,
    is_, ir, ws, wr, z1s, z1r, z2s, z2r, as_, ar, os_, or_,
):
    pipe, ctx = lax.axis_index("pipe"), lax.axis_index("ctx")
    z, x = ctx // 2, lax.rem(ctx, 2)
    y = 1 - x
    mate = {"ctx": 2 * z + y}
    following, before = lax.rem(pipe + 1, 16), lax.rem(pipe + 15, 16)
    mine = pl.multiple_of(x * HALF, HALF)
    theirs = pl.multiple_of(y * HALF, HALF)

    def level(d):
        return lax.rem(z + d, Z)

    def at_level(zz):
        return {"ctx": 2 * zz + x}

    barrier = pltpu.get_barrier_semaphore()

    def greet(d, carry):
        pl.semaphore_signal(barrier, inc=1, device_id=at_level(level(d)), device_id_type=MESH)
        return carry

    pl.semaphore_signal(barrier, inc=1, device_id=mate, device_id_type=MESH)
    lax.fori_loop(1, Z, greet, 0)
    for b in range(2):
        for p in (following, before):
            pl.semaphore_signal(
                barrier, inc=1, device_id={"pipe": p, "ctx": 2 * z + b}, device_id_type=MESH
            )

    floats = x_ref[...].astype(F32)
    scale = lax.rsqrt(jnp.mean(floats * floats, axis=-1, keepdims=True) + EPS_RMS)
    iv[x] = jnp.broadcast_to(scale, (ROWS, HEAD))
    xh[x] = x_ref[:, pl.ds(mine, HALF)]
    ldh[x] = ld_ref[pl.ds(pl.multiple_of(x * OWN, OWN), OWN), :]
    wz[z, pl.ds(pl.multiple_of(x * 64, 64), 64)] = w_ref[:, pl.ds(mine, HALF)]

    pl.semaphore_wait(barrier, Z + 4)

    first = [
        remote(x_ref.at[:, pl.ds(theirs, HALF)], xh.at[x], is_.at[0], ir.at[0], mate),
        remote(
            ld_ref.at[pl.ds(pl.multiple_of(y * OWN, OWN), OWN)], ldh.at[x], is_.at[1], ir.at[1], mate
        ),
        remote(iv.at[x], iv.at[x], is_.at[2], ir.at[2], mate),
        remote(
            w_ref.at[:, pl.ds(theirs, HALF)],
            wz.at[z, pl.ds(pl.multiple_of(x * 64, 64), 64)],
            is_.at[3], ir.at[3], mate,
        ),
    ]
    for i in (3, 1, 2, 0):
        first[i].start()

    def ring_copy(way, step, u):
        block = level(Z - step) if way == 0 else level(step)
        rows = pl.ds(u * SUB, SUB)
        return remote(
            wz.at[block, rows], wz.at[block, rows], ws.at[way, step, u], wr.at[way, step, u],
            at_level(level(1 if way == 0 else Z - 1)),
        )

    def used(way, step, u):
        return step < 7 or (u < SUBS // 2) == (way == 0)

    def arrived(way, step, u):
        block = level(Z - 1 - step) if way == 0 else level(step + 1)
        rows = pl.ds(u * SUB, SUB)
        remote(
            wz.at[block, rows], wz.at[block, rows], ws.at[way, step, u], wr.at[way, step, u],
            at_level(level(1)),
        ).wait_recv()

    def serve(step):
        for u in range(SUBS):
            for way in range(2):
                if step > 0 and used(way, step - 1, u):
                    arrived(way, step - 1, u)
                if step < 8 and used(way, step, u):
                    ring_copy(way, step, u).start()

    for b in range(2):
        row = pl.ds(2 * z + b, 1)
        ca, sa, su = coarse_ref[0, row], coarse_ref[1, row], coarse_ref[2, row]
        cs[b] = ca * fine_ref[0] - su * fine_ref[2]
        sn[b] = sa * fine_ref[0] + ca * fine_ref[1]
    rows_i = lax.broadcasted_iota(jnp.int32, (ROWS, ROWS), 0)
    cols_i = lax.broadcasted_iota(jnp.int32, (ROWS, ROWS), 1)
    lower = rows_i >= cols_i

    first[3].wait_recv()
    serve(0)
    first[1].wait_recv()
    lower_f = lower.astype(F32)
    for b in range(2):
        lds = ldh[b]
        rt[b] = dot(lds, lower_f, ((1,), (1,)), lax.Precision.HIGHEST)
        run = dot(lower_f, lds, ((1,), (1,)), lax.Precision.HIGHEST)
        for h in range(OWN):
            rb[b, h] = jnp.broadcast_to(run[:, h : h + 1], (ROWS, HEAD))
    first[2].wait_recv()
    first[0].wait_recv()

    def lanes(h):
        return pl.ds(pl.multiple_of(h * HEAD, HEAD), HEAD)

    def gain_of(ref, h):
        return ref[:, pl.ds(pl.multiple_of(x * HALF + h * HEAD, HEAD), HEAD)]

    def normed_of(b, h):
        return xh[b, :, lanes(h)].astype(F32) * iv[b]

    def rotated(u, b):
        return (u * cs[b] + pltpu.roll(u, 64, axis=1) * sn[b]).astype(BF)

    def last_of(b, h):
        return rb[b, h, ROWS - 1 : ROWS, :]

    def total_of(b, h):
        return last_of(b, h).astype(BF).astype(F32)

    def states(h, carry):
        made = []
        for b in range(2):
            normed = normed_of(b, h)
            value = normed.astype(BF)
            key = rotated(normed * gain_of(kg_ref, h), b)
            kb[b, h] = key
            vb[b, h] = value
            shrunk = (key.astype(F32) * jnp.exp(last_of(b, h) - rb[b, h])).astype(BF)
            state = dot(shrunk, value, ((0,), (0,))).astype(BF)
            made.append(state.astype(F32))
        st[h] = made[0].astype(BF)
        early, late = total_of(0, h), total_of(1, h)
        pair = (made[1] + jnp.exp(late) * made[0]).astype(BF)
        sums = jnp.concatenate(
            [jnp.broadcast_to(early, (8, HEAD)), jnp.broadcast_to(late, (8, HEAD))], axis=0
        ).astype(BF)
        for half in range(2):
            zs[2 * h + half, 0:64, :] = pair[half * 64 : half * 64 + 64]
            zs[2 * h + half, 64:80, :] = sums
        return carry

    lax.fori_loop(0, OWN // 2, states, 0)
    serve(1)
    lax.fori_loop(OWN // 2, OWN, states, 0)

    def send_pairs(d, carry):
        zz = level(d)
        remote(zs.at[zz], zr.at[z], z1s.at[zz], z1r.at[z], at_level(zz)).start()
        return carry

    lax.fori_loop(1, Z, send_pairs, 0)
    zr[z] = zs[z]

    def inside(h, carry):
        for b in range(2):
            query = rotated(normed_of(b, h) * gain_of(qg_ref, h), b)
            qb[b, h] = query
            scores = dot(query, kb[b, h], ((1,), (1,)))
            spread = rb[b, h, :, 0:1] - rt[b, pl.ds(h, 1), :]
            weight = jnp.exp(jnp.where(lower, spread, -1e30))
            inner[b, h] = dot((scores * weight).astype(BF), vb[b, h])
        return carry

    lax.fori_loop(0, OWN // 2, inside, 0)
    serve(2)
    lax.fori_loop(OWN // 2, OWN, inside, 0)
    serve(3)

    def scan(zz, state):
        @pl.when(zz != z)
        def _():
            remote(zs.at[zz], zr.at[zz], z1s.at[zz], z1r.at[zz], at_level(zz)).wait_recv()

        eo[zz] = state.astype(BF)

        @pl.when(zz != z)
        def _():
            remote(eo.at[zz], ei.at[z], z2s.at[zz], z2r.at[z], at_level(zz)).start()

        sums = zr[zz, 64:80, :].astype(F32)
        decay = jnp.exp(sums[0:1] + sums[8:9])
        return zr[zz, 0:64, :].astype(F32) + decay * state

    lax.fori_loop(0, Z, scan, jnp.zeros((64, HEAD), F32))
    ei[z] = eo[z]
    serve(4)
    serve(5)

    def head_copy(h):
        g = x * OWN + h
        slot = act.at[g // 2, :, lanes(lax.rem(g, 2))]
        return remote(slot, slot, as_.at[h], ar.at[h], mate)

    def finish(h, carry):
        for half in range(2):
            zz = 2 * h + half

            @pl.when(zz != z)
            def _():
                remote(eo.at[zz], ei.at[zz], z2s.at[zz], z2r.at[zz], at_level(zz)).wait_recv()

        entering = jnp.concatenate([ei[2 * h], ei[2 * h + 1]], axis=0)
        after = (st[h].astype(F32) + jnp.exp(total_of(0, h)) * entering.astype(F32)).astype(BF)
        g = x * OWN + h
        for b in range(2):
            carried = dot(qb[b, h], entering if b == 0 else after)
            mixed = inner[b, h] + carried * jnp.exp(rb[b, h])
            centre = mixed - jnp.mean(mixed, axis=-1, keepdims=True)
            normal = centre * lax.rsqrt(
                jnp.mean(centre * centre, axis=-1, keepdims=True) + EPS_NORM
            )
            act[g // 2, b * ROWS : (b + 1) * ROWS, lanes(lax.rem(g, 2))] = (
                normal * gain_of(og_ref, h)
            ).astype(BF)
        head_copy(h).start()
        return carry

    lax.fori_loop(0, OWN, finish, 0)
    serve(6)
    serve(7)
    serve(8)

    def partner_head(h, carry):
        g = y * OWN + h
        slot = act.at[g // 2, :, lanes(lax.rem(g, 2))]
        remote(slot, slot, as_.at[h], ar.at[h], mate).wait_recv()
        return carry

    lax.fori_loop(0, OWN, partner_head, 0)

    def out_copy(b, n):
        place = pl.ds(pl.multiple_of(x * HALF + n * COLS, COLS), COLS)
        return remote(
            ost.at[b, :, pl.ds(n * COLS, COLS)], out_ref.at[:, place],
            os_.at[b, n], or_.at[x, n], {"pipe": following, "ctx": 2 * z + b},
        )

    for n in range(PARTS):
        here = slice(n * COLS, (n + 1) * COLS)
        total = jnp.zeros((2 * ROWS, COLS), F32)
        for j in range(Z // 2):
            block = jnp.concatenate([wz[2 * j, :, here], wz[2 * j + 1, :, here]], axis=0)
            total = total + dot(act[j], block)
        for b in range(2):
            ost[b, :, here] = (
                xh[b, :, here].astype(F32) + total[b * ROWS : (b + 1) * ROWS]
            ).astype(BF)
            out_copy(b, n).start()

    for half in range(2):
        for n in range(PARTS):
            remote(
                ost.at[0, :, pl.ds(n * COLS, COLS)],
                out_ref.at[:, pl.ds(half * HALF + n * COLS, COLS)],
                os_.at[0, n], or_.at[half, n], mate,
            ).wait_recv()
    for b in range(2):
        for n in range(PARTS):
            out_copy(b, n).wait_send()
    for copy in first:
        copy.wait_send()
    for step in range(8):
        for u in range(SUBS):
            for way in range(2):
                if used(way, step, u):
                    ring_copy(way, step, u).wait_send()

    def sent(d, carry):
        zz = level(d)
        remote(zs.at[zz], zr.at[z], z1s.at[zz], z1r.at[z], at_level(zz)).wait_send()
        remote(eo.at[zz], ei.at[z], z2s.at[zz], z2r.at[z], at_level(zz)).wait_send()
        return carry

    lax.fori_loop(1, Z, sent, 0)

    def head_sent(h, carry):
        head_copy(h).wait_send()
        return carry

    lax.fori_loop(0, OWN, head_sent, 0)


def per_device(x_in, q_gain, key_gain_per_layer, out_gain, log_decay, out_weight):
    coarse, fine = (jnp.asarray(t) for t in tables())
    dma = pltpu.SemaphoreType.DMA
    vmem = pltpu.VMEM
    scratch = [
        vmem((2, ROWS, HALF), BF),
        vmem((2, ROWS, HEAD), F32),
        vmem((2, OWN, ROWS), F32),
        vmem((2, OWN, ROWS, HEAD), F32),
        vmem((2, OWN, ROWS), F32),
        vmem((2, ROWS, HEAD), F32),
        vmem((2, ROWS, HEAD), F32),
        vmem((2, OWN, ROWS, HEAD), BF),
        vmem((2, OWN, ROWS, HEAD), BF),
        vmem((2, OWN, ROWS, HEAD), BF),
        vmem((OWN, HEAD, HEAD), BF),
        vmem((2, OWN, ROWS, HEAD), F32),
        vmem((Z, 80, HEAD), BF),
        vmem((Z, 80, HEAD), BF),
        vmem((Z, 64, HEAD), BF),
        vmem((Z, 64, HEAD), BF),
        vmem((Z, 128, HALF), BF),
        vmem((Z // 2, 2 * ROWS, 2 * HEAD), BF),
        vmem((2, ROWS, HALF), BF),
        dma((4,)), dma((4,)),
        dma((2, 8, SUBS)), dma((2, 8, SUBS)),
        dma((Z,)), dma((Z,)), dma((Z,)), dma((Z,)),
        dma((OWN,)), dma((OWN,)),
        dma((2, PARTS)), dma((2, PARTS)),
    ]
    whole = pl.BlockSpec(memory_space=pltpu.VMEM)
    out = pl.pallas_call(
        kernel,
        out_shape=jax.ShapeDtypeStruct((ROWS, WIDTH), BF),
        in_specs=[whole] * 8,
        out_specs=whole,
        scratch_shapes=scratch,
        compiler_params=pltpu.CompilerParams(
            collective_id=0, has_side_effects=True, vmem_limit_bytes=48 * 2**20
        ),
        name="retention_layer",
    )(
        x_in[0, 0], q_gain, key_gain_per_layer, out_gain, log_decay[0].T, out_weight[0], coarse, fine
    )
    return out[None, None]


def solution(mesh):
    placed = (
        P("pipe", None, "ctx", None),
        P("pipe", None),
        P("pipe", None),
        P("pipe", None),
        P("pipe", "ctx", None),
        P("pipe", "ctx", None),
    )
    return jax.shard_map(
        per_device,
        mesh=mesh,
        in_specs=placed,
        out_specs=P("pipe", None, "ctx", None),
        check_vma=False,
    )
```

```python
import jax
import jax.numpy as jnp
import numpy as np
from jax import lax
from jax.experimental import pallas as pl
from jax.experimental.pallas import tpu as pltpu
from jax.sharding import PartitionSpec as P

EPS_RMS = 1e-06
EPS_NORM = 1e-05
MESH = pl.DeviceIdType.MESH
BF, F32 = jnp.bfloat16, jnp.float32
ROWS, WIDTH, HALF, HEAD, HEADS, OWN = 160, 2048, 1024, 128, 16, 8
Z, QUAD, SUBS, PARTS, COLS = 16, 4, 4, 4, 256
SUB = 128 // SUBS


def tables():
    freqs = 10000.0 ** (-2.0 * np.arange(64) / 128.0)
    freqs = np.concatenate([freqs, freqs])[None, :]
    sign = np.where(np.arange(128) < 64, -1.0, 1.0)[None, :]
    coarse = np.arange(32)[:, None] * float(ROWS) * freqs
    fine = np.arange(ROWS)[:, None] * freqs
    return tuple(
        np.stack([np.cos(a), sign * np.sin(a), np.sin(a)]).astype(np.float32) for a in (coarse, fine)
    )


def remote(src, dst, send, recv, device):
    return pltpu.make_async_remote_copy(
        src_ref=src, dst_ref=dst, send_sem=send, recv_sem=recv, device_id=device, device_id_type=MESH
    )


def dot(a, b, dims=((1,), (0,)), precision=None):
    return lax.dot_general(a, b, (dims, ((), ())), precision=precision, preferred_element_type=F32)


def kernel(
    x_hbm, qg_hbm, kg_hbm, og_hbm, ld_hbm, w_hbm, coarse_hbm, fine_hbm,
    out_ref,
    xv, gains, ldv, coarse, fine,
    xh, iv, ldh, rb, rt, cs, sn, kb, vb, qb, st, inner, zs, zr, gs, gr, eo, er, fo, ei, wz, act, acc, ost,
    ins, is_, ir, ws, wr, s1, r1, s2, r2, s3, r3, s4, r4, as_, ar, os_, or_,
):
    pipe, ctx = lax.axis_index("pipe"), lax.axis_index("ctx")
    z, x = ctx // 2, lax.rem(ctx, 2)
    quad, place = z // QUAD, lax.rem(z, QUAD)
    y = 1 - x
    mate = {"ctx": 2 * z + y}
    following, before = lax.rem(pipe + 1, 16), lax.rem(pipe + 15, 16)
    mine = pl.ds(pl.multiple_of(x * HALF, HALF), HALF)
    theirs = pl.ds(pl.multiple_of(y * HALF, HALF), HALF)

    def level(d):
        return lax.rem(z + d, Z)

    def at_level(zz):
        return {"ctx": 2 * zz + x}

    def at_place(p):
        return at_level(quad * QUAD + p)

    def at_quad(q):
        return at_level(q * QUAD + place)

    barrier = pltpu.get_barrier_semaphore()
    greeted = [mate, at_level(level(1)), at_level(level(Z - 1))]
    for d in range(1, QUAD):
        greeted.append(at_place(lax.rem(place + d, QUAD)))
        greeted.append(at_quad(lax.rem(quad + d, QUAD)))
    for b in range(2):
        for p in (following, before):
            greeted.append({"pipe": p, "ctx": 2 * z + b})
    for device in greeted:
        pl.semaphore_signal(barrier, inc=1, device_id=device, device_id_type=MESH)

    own_rows = pl.ds(pl.multiple_of(x * 64, 64), 64)
    fetches = [
        pltpu.make_async_copy(w_hbm.at[:, mine], wz.at[z, own_rows], ins.at[0]),
        pltpu.make_async_copy(x_hbm, xv, ins.at[1]),
        pltpu.make_async_copy(ld_hbm, ldv, ins.at[2]),
        pltpu.make_async_copy(coarse_hbm, coarse, ins.at[3]),
        pltpu.make_async_copy(fine_hbm, fine, ins.at[4]),
        pltpu.make_async_copy(kg_hbm.at[:, mine], gains.at[0], ins.at[5]),
        pltpu.make_async_copy(qg_hbm.at[:, mine], gains.at[1], ins.at[6]),
        pltpu.make_async_copy(og_hbm.at[:, mine], gains.at[2], ins.at[7]),
    ]
    for fetch in fetches:
        fetch.start()

    fetches[1].wait()
    floats = xv[...].astype(F32)
    scale = lax.rsqrt(jnp.mean(floats * floats, axis=-1, keepdims=True) + EPS_RMS)
    iv[x] = jnp.broadcast_to(scale, (ROWS, HEAD))
    xh[x] = xv[:, mine]
    fetches[2].wait()
    ldh[x] = ldv[pl.ds(pl.multiple_of(x * OWN, OWN), OWN), :]
    fetches[0].wait()

    pl.semaphore_wait(barrier, len(greeted))

    def ring_copy(way, step, k, came):
        block = level(Z - step - came) if way == 0 else level(step + came)
        rows = pl.ds(pl.multiple_of(lax.rem(2 * x + k, SUBS) * SUB, SUB), SUB)
        return remote(
            wz.at[block, rows], wz.at[block, rows], ws.at[way, step, k], wr.at[way, step, k],
            at_level(level(1 if way == 0 else Z - 1)),
        )

    def used(way, step, k):
        return step < 7 or (k < SUBS // 2) == (way == 0)

    def serve(step, parts=range(SUBS)):
        for k in parts:
            for way in range(2):
                if step > 0 and used(way, step - 1, k):
                    ring_copy(way, step - 1, k, 1).wait_recv()
                if step < 8 and used(way, step, k):
                    ring_copy(way, step, k, 0).start()

    first = [
        remote(w_hbm.at[:, theirs], wz.at[z, own_rows], is_.at[0], ir.at[0], mate),
        remote(
            ldv.at[pl.ds(pl.multiple_of(y * OWN, OWN), OWN)], ldh.at[x], is_.at[1], ir.at[1], mate
        ),
        remote(iv.at[x], iv.at[x], is_.at[2], ir.at[2], mate),
        remote(xv.at[:, theirs], xh.at[x], is_.at[3], ir.at[3], mate),
    ]
    first[0].start()
    serve(0, (0, 1))
    for copy in first[1:]:
        copy.start()

    fetches[3].wait()
    fetches[4].wait()
    for b in range(2):
        row = pl.ds(2 * z + b, 1)
        ca, sa, su = coarse[0, row], coarse[1, row], coarse[2, row]
        cs[b] = ca * fine[0] - su * fine[2]
        sn[b] = sa * fine[0] + ca * fine[1]
    rows_i = lax.broadcasted_iota(jnp.int32, (ROWS, ROWS), 0)
    cols_i = lax.broadcasted_iota(jnp.int32, (ROWS, ROWS), 1)
    lower = rows_i >= cols_i
    lower_f = lower.astype(F32)
    for i in (5, 6, 7):
        fetches[i].wait()

    first[0].wait_recv()
    serve(0, (2, 3))
    first[1].wait_recv()
    for b in range(2):
        lds = ldh[b]
        rt[b] = dot(lds, lower_f, ((1,), (1,)), lax.Precision.HIGHEST)
        run = dot(lower_f, lds, ((1,), (1,)), lax.Precision.HIGHEST)
        for h in range(OWN):
            rb[b, h] = jnp.broadcast_to(run[:, h : h + 1], (ROWS, HEAD))
    first[2].wait_recv()
    first[3].wait_recv()

    def lanes(h):
        return pl.ds(pl.multiple_of(h * HEAD, HEAD), HEAD)

    def normed_of(b, h):
        return xh[b, :, lanes(h)].astype(F32) * iv[b]

    def rotated(u, b):
        return (u * cs[b] + pltpu.roll(u, 64, axis=1) * sn[b]).astype(BF)

    def last_of(b, h):
        return rb[b, h, ROWS - 1 : ROWS, :]

    def total_of(b, h):
        return last_of(b, h).astype(BF).astype(F32)

    def two_rows(above, below):
        return jnp.concatenate(
            [jnp.broadcast_to(above, (8, HEAD)), jnp.broadcast_to(below, (8, HEAD))], axis=0
        ).astype(BF)

    def states(h):
        made = []
        for b in range(2):
            normed = normed_of(b, h)
            value = normed.astype(BF)
            key = rotated(normed * gains[0, :, lanes(h)], b)
            kb[b, h] = key
            vb[b, h] = value
            shrunk = (key.astype(F32) * jnp.exp(last_of(b, h) - rb[b, h])).astype(BF)
            state = dot(shrunk, value, ((0,), (0,))).astype(BF)
            made.append(state.astype(F32))
        st[h] = made[0].astype(BF)
        early, late = total_of(0, h), total_of(1, h)
        zs[h, 0:HEAD, :] = (made[1] + jnp.exp(late) * made[0]).astype(BF)
        zs[h, HEAD : HEAD + 16, :] = two_rows(early, late)

    def pair_copy(p, came):
        return remote(
            zs.at[pl.ds(2 * p, 2)], zr.at[p if came else place], s1.at[p], r1.at[p if came else place],
            at_place(p),
        )

    def states_for(d, carry):
        p = lax.rem(place + d, QUAD)
        states(2 * p)
        states(2 * p + 1)

        @pl.when(d < QUAD)
        def _():
            pair_copy(p, False).start()

        return carry

    lax.fori_loop(1, QUAD + 1, states_for, 0)
    zr[place] = zs[pl.ds(2 * place, 2)]
    serve(1)

    def inside(h, carry):
        for b in range(2):
            query = rotated(normed_of(b, h) * gains[1, :, lanes(h)], b)
            qb[b, h] = query
            scores = dot(query, kb[b, h], ((1,), (1,)))
            spread = rb[b, h, :, 0:1] - rt[b, pl.ds(h, 1), :]
            weight = jnp.exp(jnp.where(lower, spread, -1e30))
            inner[b, h] = dot((scores * weight).astype(BF), vb[b, h])
        return carry

    lax.fori_loop(0, OWN, inside, 0)
    serve(2)

    def unless(p, own, thing):
        @pl.when(p != own)
        def _():
            thing()

    for p in range(QUAD):
        unless(p, place, lambda: pair_copy(p, True).wait_recv())

    def decay_of(p, i):
        sums = zr[p, i, HEAD : HEAD + 16, :].astype(F32)
        return sums[0:1] + sums[8:9]

    for i in range(2):
        state = zr[0, i, 0:HEAD, :].astype(F32)
        span = decay_of(0, i)
        for p in range(1, QUAD):
            now = decay_of(p, i)
            state = zr[p, i, 0:HEAD, :].astype(F32) + jnp.exp(now) * state
            span = span + now
        coarse_span = span.astype(BF).astype(F32)
        for half in range(2):
            gs[2 * i + half, 0:64, :] = state[half * 64 : half * 64 + 64].astype(BF)
            gs[2 * i + half, 64:80, :] = two_rows(coarse_span, span - coarse_span)

    def quad_copy(q, came):
        return remote(
            gs.at[q], gr.at[q if came else quad], s2.at[q], r2.at[q if came else quad], at_quad(q)
        )

    for q in range(QUAD):
        unless(q, quad, lambda: quad_copy(q, False).start())
    gr[quad] = gs[quad]
    serve(3)

    def back_copy(q, came):
        return remote(
            eo.at[q], er.at[q if came else quad], s3.at[q], r3.at[q if came else quad], at_quad(q)
        )

    state = jnp.zeros((64, HEAD), F32)
    for q in range(QUAD):
        eo[q] = state.astype(BF)
        unless(q, quad, lambda: back_copy(q, False).start())
        if q < QUAD - 1:
            unless(q, quad, lambda: quad_copy(q, True).wait_recv())
            sums = gr[q, 64:80, :].astype(F32)
            state = gr[q, 0:64, :].astype(F32) + jnp.exp(sums[0:1] + sums[8:9]) * state
    er[quad] = eo[quad]
    unless(QUAD - 1, quad, lambda: quad_copy(QUAD - 1, True).wait_recv())
    serve(4)

    def enter_copy(p, came):
        return remote(
            fo.at[p], ei.at[p if came else place], s4.at[p], r4.at[p if came else place], at_place(p)
        )

    for q in range(QUAD):
        unless(q, quad, lambda: back_copy(q, True).wait_recv())
    entry = [
        jnp.concatenate([er[2 * i], er[2 * i + 1]], axis=0).astype(F32) for i in range(2)
    ]
    for p in range(QUAD):
        for i in range(2):
            fo[p, i] = entry[i].astype(BF)
            if p < QUAD - 1:
                entry[i] = zr[p, i, 0:HEAD, :].astype(F32) + jnp.exp(decay_of(p, i)) * entry[i]
        unless(p, place, lambda: enter_copy(p, False).start())
    ei[place] = fo[place]
    serve(5)

    def head_copy(h, came):
        g = (y if came else x) * OWN + h
        return remote(act.at[g], act.at[g], as_.at[h], ar.at[h], mate)

    def finish(h, p, i):
        entering = ei[p, i]
        after = (st[h].astype(F32) + jnp.exp(total_of(0, h)) * entering.astype(F32)).astype(BF)
        for b in range(2):
            carried = dot(qb[b, h], entering if b == 0 else after)
            mixed = inner[b, h] + carried * jnp.exp(rb[b, h])
            centre = mixed - jnp.mean(mixed, axis=-1, keepdims=True)
            normal = centre * lax.rsqrt(
                jnp.mean(centre * centre, axis=-1, keepdims=True) + EPS_NORM
            )
            act[x * OWN + h, b * ROWS : (b + 1) * ROWS, :] = (
                normal * gains[2, :, lanes(h)]
            ).astype(BF)
        head_copy(h, False).start()

    def finish_of(d, carry):
        p = lax.rem(place + d, QUAD)

        @pl.when(d > 0)
        def _():
            enter_copy(p, True).wait_recv()

        for i in range(2):
            finish(2 * p + i, p, i)
        return carry

    lax.fori_loop(0, QUAD, finish_of, 0)
    serve(6)

    def partner_head(h, carry):
        head_copy(h, True).wait_recv()
        return carry

    lax.fori_loop(0, OWN, partner_head, 0)
    serve(7)

    def product(n, one, two):
        here = slice(n * COLS, (n + 1) * COLS)
        left = jnp.concatenate([act[one], act[two]], axis=1)
        right = jnp.concatenate([wz[one, :, here], wz[two, :, here]], axis=0)
        return dot(left, right)

    for n in range(PARTS):
        total = product(n, level(1), level(Z - 1))
        for d in range(2, Z // 2):
            total = total + product(n, level(d), level(Z - d))
        acc[n] = total
    serve(8)

    def out_copy(b, n):
        there = pl.ds(pl.multiple_of(x * HALF + n * COLS, COLS), COLS)
        return remote(
            ost.at[b, n], out_ref.at[:, there],
            os_.at[b, n], or_.at[x, n], {"pipe": following, "ctx": 2 * z + b},
        )

    for n in range(PARTS):
        here = slice(n * COLS, (n + 1) * COLS)
        total = acc[n] + product(n, z, level(Z // 2))
        for b in range(2):
            ost[b, n] = (
                xh[b, :, here].astype(F32) + total[b * ROWS : (b + 1) * ROWS]
            ).astype(BF)
            out_copy(b, n).start()

    for copy in first:
        copy.wait_send()
    for step in range(8):
        for k in range(SUBS):
            for way in range(2):
                if used(way, step, k):
                    ring_copy(way, step, k, 0).wait_send()
    for p in range(QUAD):
        unless(p, place, lambda: pair_copy(p, False).wait_send())
        unless(p, quad, lambda: quad_copy(p, False).wait_send())
        unless(p, quad, lambda: back_copy(p, False).wait_send())
        unless(p, place, lambda: enter_copy(p, False).wait_send())

    def head_sent(h, carry):
        head_copy(h, False).wait_send()
        return carry

    lax.fori_loop(0, OWN, head_sent, 0)
    for n in range(PARTS):
        for half in range(2):
            remote(
                ost.at[0, n], out_ref.at[:, pl.ds(half * HALF + n * COLS, COLS)],
                os_.at[0, n], or_.at[half, n], mate,
            ).wait_recv()
        for b in range(2):
            out_copy(b, n).wait_send()


def per_device(x_in, q_gain, key_gain_per_layer, out_gain, log_decay, out_weight):
    coarse, fine = (jnp.asarray(t) for t in tables())
    dma = pltpu.SemaphoreType.DMA
    vmem = pltpu.VMEM
    scratch = [
        vmem((ROWS, WIDTH), BF),
        vmem((3, 1, HALF), F32),
        vmem((HEADS, ROWS), F32),
        vmem((3, 32, HEAD), F32),
        vmem((3, ROWS, HEAD), F32),
        vmem((2, ROWS, HALF), BF),
        vmem((2, ROWS, HEAD), F32),
        vmem((2, OWN, ROWS), F32),
        vmem((2, OWN, ROWS, HEAD), F32),
        vmem((2, OWN, ROWS), F32),
        vmem((2, ROWS, HEAD), F32),
        vmem((2, ROWS, HEAD), F32),
        vmem((2, OWN, ROWS, HEAD), BF),
        vmem((2, OWN, ROWS, HEAD), BF),
        vmem((2, OWN, ROWS, HEAD), BF),
        vmem((OWN, HEAD, HEAD), BF),
        vmem((2, OWN, ROWS, HEAD), F32),
        vmem((OWN, HEAD + 16, HEAD), BF),
        vmem((QUAD, 2, HEAD + 16, HEAD), BF),
        vmem((QUAD, 80, HEAD), BF),
        vmem((QUAD, 80, HEAD), BF),
        vmem((QUAD, 64, HEAD), BF),
        vmem((QUAD, 64, HEAD), BF),
        vmem((QUAD, 2, HEAD, HEAD), BF),
        vmem((QUAD, 2, HEAD, HEAD), BF),
        vmem((Z, 128, HALF), BF),
        vmem((HEADS, 2 * ROWS, HEAD), BF),
        vmem((PARTS, 2 * ROWS, COLS), F32),
        vmem((2, PARTS, ROWS, COLS), BF),
        dma((8,)),
        dma((4,)), dma((4,)),
        dma((2, 8, SUBS)), dma((2, 8, SUBS)),
        *(dma((QUAD,)) for _ in range(8)),
        dma((OWN,)), dma((OWN,)),
        dma((2, PARTS)), dma((2, PARTS)),
    ]
    whole = pl.BlockSpec(memory_space=pltpu.VMEM)
    out = pl.pallas_call(
        kernel,
        out_shape=jax.ShapeDtypeStruct((ROWS, WIDTH), BF),
        in_specs=[pl.BlockSpec(memory_space=pltpu.HBM)] * 8,
        out_specs=whole,
        scratch_shapes=scratch,
        compiler_params=pltpu.CompilerParams(
            collective_id=0, has_side_effects=True, vmem_limit_bytes=64 * 2**20 - 2**16
        ),
        name="retention_layer",
    )(
        x_in[0, 0], q_gain, key_gain_per_layer, out_gain, log_decay[0].T, out_weight[0], coarse, fine
    )
    return out[None, None]


def solution(mesh):
    placed = (
        P("pipe", None, "ctx", None),
        P("pipe", None),
        P("pipe", None),
        P("pipe", None),
        P("pipe", "ctx", None),
        P("pipe", "ctx", None),
    )
    return jax.shard_map(
        per_device,
        mesh=mesh,
        in_specs=placed,
        out_specs=P("pipe", None, "ctx", None),
        check_vma=False,
    )
```

```python
import jax
import jax.numpy as jnp
import numpy as np
from jax import lax
from jax.experimental import pallas as pl
from jax.experimental.pallas import tpu as pltpu
from jax.sharding import PartitionSpec as P

EPS_RMS = 1e-06
EPS_NORM = 1e-05
MESH = pl.DeviceIdType.MESH
BF, F32 = jnp.bfloat16, jnp.float32
ROWS, WIDTH, HALF, HEAD, HEADS, OWN = 160, 2048, 1024, 128, 16, 8
Z, QUAD, SUBS, PARTS, COLS = 16, 4, 4, 4, 256
SUB = 128 // SUBS


def tables():
    freqs = 10000.0 ** (-2.0 * np.arange(64) / 128.0)
    freqs = np.concatenate([freqs, freqs])[None, :]
    sign = np.where(np.arange(128) < 64, -1.0, 1.0)[None, :]
    coarse = np.arange(32)[:, None] * float(ROWS) * freqs
    fine = np.arange(ROWS)[:, None] * freqs
    return tuple(
        np.stack([np.cos(a), sign * np.sin(a), np.sin(a)]).astype(np.float32) for a in (coarse, fine)
    )


def remote(src, dst, send, recv, device):
    return pltpu.make_async_remote_copy(
        src_ref=src, dst_ref=dst, send_sem=send, recv_sem=recv, device_id=device, device_id_type=MESH
    )


def dot(a, b, dims=((1,), (0,)), precision=None):
    return lax.dot_general(a, b, (dims, ((), ())), precision=precision, preferred_element_type=F32)


def kernel(
    x_hbm, qg_hbm, kg_hbm, og_hbm, ld_hbm, w_hbm, coarse_hbm, fine_hbm,
    out_ref,
    xv, gains, ldv, coarse, fine,
    xh, iv, sm, ldh, rb, rt, cs, sn, kb, vb, qb, st, inner, zs, zr, gs, gr, eo, er, fo, ei, wz, act, acc, ost,
    ins, is_, ir, ws, wr, s1, r1, s2, r2, s3, r3, s4, r4, as_, ar, os_, or_,
):
    pipe, ctx = lax.axis_index("pipe"), lax.axis_index("ctx")
    z, x = ctx // 2, lax.rem(ctx, 2)
    quad, place = z // QUAD, lax.rem(z, QUAD)
    y = 1 - x
    mate = {"ctx": 2 * z + y}
    following, before = lax.rem(pipe + 1, 16), lax.rem(pipe + 15, 16)
    mine = pl.ds(pl.multiple_of(x * HALF, HALF), HALF)
    theirs = pl.ds(pl.multiple_of(y * HALF, HALF), HALF)

    def level(d):
        return lax.rem(z + d, Z)

    def at_level(zz):
        return {"ctx": 2 * zz + x}

    def at_place(p):
        return at_level(quad * QUAD + p)

    def at_quad(q):
        return at_level(q * QUAD + place)

    barrier = pltpu.get_barrier_semaphore()
    greeted = [mate, at_level(level(1)), at_level(level(Z - 1))]
    for d in range(1, QUAD):
        greeted.append(at_place(lax.rem(place + d, QUAD)))
        greeted.append(at_quad(lax.rem(quad + d, QUAD)))
    for b in range(2):
        for p in (following, before):
            greeted.append({"pipe": p, "ctx": 2 * z + b})
    for device in greeted:
        pl.semaphore_signal(barrier, inc=1, device_id=device, device_id_type=MESH)

    own_rows = pl.ds(pl.multiple_of(x * 64, 64), 64)
    fetches = [
        pltpu.make_async_copy(w_hbm.at[:, mine], wz.at[z, own_rows], ins.at[0]),
        pltpu.make_async_copy(x_hbm, xv, ins.at[1]),
        pltpu.make_async_copy(ld_hbm, ldv, ins.at[2]),
        pltpu.make_async_copy(coarse_hbm, coarse, ins.at[3]),
        pltpu.make_async_copy(fine_hbm, fine, ins.at[4]),
        pltpu.make_async_copy(kg_hbm.at[:, mine], gains.at[0], ins.at[5]),
        pltpu.make_async_copy(qg_hbm.at[:, mine], gains.at[1], ins.at[6]),
        pltpu.make_async_copy(og_hbm.at[:, mine], gains.at[2], ins.at[7]),
    ]
    for fetch in fetches:
        fetch.start()

    fetches[1].wait()
    floats = xv[...].astype(F32)
    scale = lax.rsqrt(jnp.mean(floats * floats, axis=-1, keepdims=True) + EPS_RMS)
    iv[x] = jnp.broadcast_to(scale, (ROWS, HEAD))
    xh[x] = xv[:, mine]
    rows_i = lax.broadcasted_iota(jnp.int32, (ROWS, ROWS), 0)
    cols_i = lax.broadcasted_iota(jnp.int32, (ROWS, ROWS), 1)
    lower = rows_i >= cols_i
    lower_f = lower.astype(F32)
    same = rows_i == cols_i
    exact = lax.Precision.HIGHEST
    sm[OWN : 2 * OWN, :] = dot(
        jnp.ones((8, ROWS), F32), jnp.where(same, scale, 0.0), precision=exact
    )
    fetches[2].wait()
    ldh[x, 0:OWN, :] = ldv[pl.ds(pl.multiple_of(x * OWN, OWN), OWN), :]
    sm[0:OWN, :] = ldv[pl.ds(pl.multiple_of(y * OWN, OWN), OWN), :]
    fetches[0].wait()

    pl.semaphore_wait(barrier, len(greeted))

    def ring_copy(way, step, k, came):
        block = level(Z - step - came) if way == 0 else level(step + came)
        rows = pl.ds(pl.multiple_of(lax.rem(2 * x + k, SUBS) * SUB, SUB), SUB)
        return remote(
            wz.at[block, rows], wz.at[block, rows], ws.at[way, step, k], wr.at[way, step, k],
            at_level(level(1 if way == 0 else Z - 1)),
        )

    def used(way, step, k):
        return step < 7 or (k < SUBS // 2) == (way == 0)

    def serve(step, parts=range(SUBS)):
        for k in parts:
            for way in range(2):
                if step > 0 and used(way, step - 1, k):
                    ring_copy(way, step - 1, k, 1).wait_recv()
                if step < 8 and used(way, step, k):
                    ring_copy(way, step, k, 0).start()

    first = [
        remote(w_hbm.at[:, theirs], wz.at[z, own_rows], is_.at[0], ir.at[0], mate),
        remote(sm, ldh.at[x], is_.at[1], ir.at[1], mate),
        remote(xv.at[:, theirs], xh.at[x], is_.at[2], ir.at[2], mate),
    ]
    first[0].start()
    serve(0, (0, 1))
    for copy in first[1:]:
        copy.start()

    fetches[3].wait()
    fetches[4].wait()
    for b in range(2):
        row = pl.ds(2 * z + b, 1)
        ca, sa, su = coarse[0, row], coarse[1, row], coarse[2, row]
        cs[b] = ca * fine[0] - su * fine[2]
        sn[b] = sa * fine[0] + ca * fine[1]
    for i in (5, 6, 7):
        fetches[i].wait()

    def sums_of(b):
        lds = ldh[b, 0:OWN, :]
        rt[b] = dot(lds, lower_f, ((1,), (1,)), exact)
        run = dot(lower_f, lds, ((1,), (1,)), exact)
        for h in range(OWN):
            rb[b, h] = jnp.broadcast_to(run[:, h : h + 1], (ROWS, HEAD))

    def lanes(h):
        return pl.ds(pl.multiple_of(h * HEAD, HEAD), HEAD)

    def normed_of(b, h):
        return xh[b, :, lanes(h)].astype(F32) * iv[b]

    def rotated(u, b):
        return (u * cs[b] + pltpu.roll(u, 64, axis=1) * sn[b]).astype(BF)

    def last_of(b, h):
        return rb[b, h, ROWS - 1 : ROWS, :]

    def total_of(b, h):
        return last_of(b, h).astype(BF).astype(F32)

    def two_rows(above, below):
        return jnp.concatenate(
            [jnp.broadcast_to(above, (8, HEAD)), jnp.broadcast_to(below, (8, HEAD))], axis=0
        ).astype(BF)

    def states(b, h):
        normed = normed_of(b, h)
        value = normed.astype(BF)
        key = rotated(normed * gains[0, :, lanes(h)], b)
        kb[b, h] = key
        vb[b, h] = value
        shrunk = (key.astype(F32) * jnp.exp(last_of(b, h) - rb[b, h])).astype(BF)
        st[b, h] = dot(shrunk, value, ((0,), (0,))).astype(BF)

    def inside(b, h):
        query = rotated(normed_of(b, h) * gains[1, :, lanes(h)], b)
        qb[b, h] = query
        scores = dot(query, kb[b, h], ((1,), (1,)))
        spread = rb[b, h, :, 0:1] - rt[b, pl.ds(h, 1), :]
        weight = jnp.exp(jnp.where(lower, spread, -1e30))
        inner[b, h] = dot((scores * weight).astype(BF), vb[b, h])

    def over_heads(thing, b, start, stop):
        def step(i, carry):
            thing(b, 2 * i)
            thing(b, 2 * i + 1)
            return carry

        lax.fori_loop(start // 2, stop // 2, step, 0)

    sums_of(x)
    over_heads(states, x, 0, OWN)
    first[0].wait_recv()
    serve(0, (2, 3))
    over_heads(inside, x, 0, OWN // 2)
    serve(1, (0, 1))
    over_heads(inside, x, OWN // 2, OWN)
    first[1].wait_recv()
    sums_of(y)
    iv[y] = dot(
        jnp.where(same, ldh[y, OWN : OWN + 1, :], 0.0), jnp.ones((ROWS, HEAD), F32), precision=exact
    )
    serve(1, (2, 3))
    first[2].wait_recv()

    def pair_copy(p, came):
        return remote(
            zs.at[pl.ds(2 * p, 2)], zr.at[p if came else place], s1.at[p], r1.at[p if came else place],
            at_place(p),
        )

    def pair_states(h):
        states(y, h)
        early, late = total_of(0, h), total_of(1, h)
        zs[h, 0:HEAD, :] = (
            st[1, h].astype(F32) + jnp.exp(late) * st[0, h].astype(F32)
        ).astype(BF)
        zs[h, HEAD : HEAD + 16, :] = two_rows(early, late)

    def states_for(d, carry):
        p = lax.rem(place + d, QUAD)
        pair_states(2 * p)
        pair_states(2 * p + 1)

        @pl.when(d < QUAD)
        def _():
            pair_copy(p, False).start()

        return carry

    lax.fori_loop(1, QUAD + 1, states_for, 0)
    zr[place] = zs[pl.ds(2 * place, 2)]
    serve(2, (0, 1))
    over_heads(inside, y, 0, OWN // 2)
    serve(2, (2, 3))
    over_heads(inside, y, OWN // 2, OWN)

    def unless(p, own, thing):
        @pl.when(p != own)
        def _():
            thing()

    for p in range(QUAD):
        unless(p, place, lambda: pair_copy(p, True).wait_recv())

    def decay_of(p, i):
        sums = zr[p, i, HEAD : HEAD + 16, :].astype(F32)
        return sums[0:1] + sums[8:9]

    for i in range(2):
        state = zr[0, i, 0:HEAD, :].astype(F32)
        span = decay_of(0, i)
        for p in range(1, QUAD):
            now = decay_of(p, i)
            state = zr[p, i, 0:HEAD, :].astype(F32) + jnp.exp(now) * state
            span = span + now
        coarse_span = span.astype(BF).astype(F32)
        for half in range(2):
            gs[2 * i + half, 0:64, :] = state[half * 64 : half * 64 + 64].astype(BF)
            gs[2 * i + half, 64:80, :] = two_rows(coarse_span, span - coarse_span)

    def quad_copy(q, came):
        return remote(
            gs.at[q], gr.at[q if came else quad], s2.at[q], r2.at[q if came else quad], at_quad(q)
        )

    for q in range(QUAD):
        unless(q, quad, lambda: quad_copy(q, False).start())
    gr[quad] = gs[quad]
    serve(3)

    def back_copy(q, came):
        return remote(
            eo.at[q], er.at[q if came else quad], s3.at[q], r3.at[q if came else quad], at_quad(q)
        )

    state = jnp.zeros((64, HEAD), F32)
    for q in range(QUAD):
        eo[q] = state.astype(BF)
        unless(q, quad, lambda: back_copy(q, False).start())
        if q < QUAD - 1:
            unless(q, quad, lambda: quad_copy(q, True).wait_recv())
            sums = gr[q, 64:80, :].astype(F32)
            state = gr[q, 0:64, :].astype(F32) + jnp.exp(sums[0:1] + sums[8:9]) * state
    er[quad] = eo[quad]
    unless(QUAD - 1, quad, lambda: quad_copy(QUAD - 1, True).wait_recv())
    serve(4)

    def enter_copy(p, came):
        return remote(
            fo.at[p], ei.at[p if came else place], s4.at[p], r4.at[p if came else place], at_place(p)
        )

    for q in range(QUAD):
        unless(q, quad, lambda: back_copy(q, True).wait_recv())
    entry = [
        jnp.concatenate([er[2 * i], er[2 * i + 1]], axis=0).astype(F32) for i in range(2)
    ]
    for p in range(QUAD):
        for i in range(2):
            fo[p, i] = entry[i].astype(BF)
            if p < QUAD - 1:
                entry[i] = zr[p, i, 0:HEAD, :].astype(F32) + jnp.exp(decay_of(p, i)) * entry[i]
        unless(p, place, lambda: enter_copy(p, False).start())
    ei[place] = fo[place]
    serve(5)

    def head_copy(h, came):
        g = (y if came else x) * OWN + h
        return remote(act.at[g], act.at[g], as_.at[h], ar.at[h], mate)

    def finish(h, p, i):
        entering = ei[p, i]
        after = (st[0, h].astype(F32) + jnp.exp(total_of(0, h)) * entering.astype(F32)).astype(BF)
        for b in range(2):
            carried = dot(qb[b, h], entering if b == 0 else after)
            mixed = inner[b, h] + carried * jnp.exp(rb[b, h])
            centre = mixed - jnp.mean(mixed, axis=-1, keepdims=True)
            normal = centre * lax.rsqrt(
                jnp.mean(centre * centre, axis=-1, keepdims=True) + EPS_NORM
            )
            act[x * OWN + h, b * ROWS : (b + 1) * ROWS, :] = (
                normal * gains[2, :, lanes(h)]
            ).astype(BF)
        head_copy(h, False).start()

    def finish_of(d, carry):
        p = lax.rem(place + d, QUAD)

        @pl.when(d > 0)
        def _():
            enter_copy(p, True).wait_recv()

        for i in range(2):
            finish(2 * p + i, p, i)
        return carry

    lax.fori_loop(0, QUAD, finish_of, 0)
    serve(6)

    def partner_head(h, carry):
        head_copy(h, True).wait_recv()
        return carry

    serve(7)
    lax.fori_loop(0, OWN, partner_head, 0)

    def product(n, one, two):
        here = slice(n * COLS, (n + 1) * COLS)
        left = jnp.concatenate([act[one], act[two]], axis=1)
        right = jnp.concatenate([wz[one, :, here], wz[two, :, here]], axis=0)
        return dot(left, right)

    for n in range(PARTS):
        total = product(n, level(1), level(Z - 1))
        for d in range(2, Z // 2):
            total = total + product(n, level(d), level(Z - d))
        acc[n] = total
    serve(8)

    def out_copy(b, n):
        there = pl.ds(pl.multiple_of(x * HALF + n * COLS, COLS), COLS)
        return remote(
            ost.at[b, n], out_ref.at[:, there],
            os_.at[b, n], or_.at[x, n], {"pipe": following, "ctx": 2 * z + b},
        )

    for n in range(PARTS):
        here = slice(n * COLS, (n + 1) * COLS)
        total = acc[n] + product(n, z, level(Z // 2))
        for b in range(2):
            ost[b, n] = (
                xh[b, :, here].astype(F32) + total[b * ROWS : (b + 1) * ROWS]
            ).astype(BF)
            out_copy(b, n).start()

    for copy in first:
        copy.wait_send()
    for step in range(8):
        for k in range(SUBS):
            for way in range(2):
                if used(way, step, k):
                    ring_copy(way, step, k, 0).wait_send()
    for p in range(QUAD):
        unless(p, place, lambda: pair_copy(p, False).wait_send())
        unless(p, quad, lambda: quad_copy(p, False).wait_send())
        unless(p, quad, lambda: back_copy(p, False).wait_send())
        unless(p, place, lambda: enter_copy(p, False).wait_send())

    def head_sent(h, carry):
        head_copy(h, False).wait_send()
        return carry

    lax.fori_loop(0, OWN, head_sent, 0)
    for n in range(PARTS):
        for half in range(2):
            remote(
                ost.at[0, n], out_ref.at[:, pl.ds(half * HALF + n * COLS, COLS)],
                os_.at[0, n], or_.at[half, n], mate,
            ).wait_recv()
        for b in range(2):
            out_copy(b, n).wait_send()


def per_device(x_in, q_gain, key_gain_per_layer, out_gain, log_decay, out_weight):
    coarse, fine = (jnp.asarray(t) for t in tables())
    dma = pltpu.SemaphoreType.DMA
    vmem = pltpu.VMEM
    scratch = [
        vmem((ROWS, WIDTH), BF),
        vmem((3, 1, HALF), F32),
        vmem((HEADS, ROWS), F32),
        vmem((3, 32, HEAD), F32),
        vmem((3, ROWS, HEAD), F32),
        vmem((2, ROWS, HALF), BF),
        vmem((2, ROWS, HEAD), F32),
        vmem((2 * OWN, ROWS), F32),
        vmem((2, 2 * OWN, ROWS), F32),
        vmem((2, OWN, ROWS, HEAD), F32),
        vmem((2, OWN, ROWS), F32),
        vmem((2, ROWS, HEAD), F32),
        vmem((2, ROWS, HEAD), F32),
        vmem((2, OWN, ROWS, HEAD), BF),
        vmem((2, OWN, ROWS, HEAD), BF),
        vmem((2, OWN, ROWS, HEAD), BF),
        vmem((2, OWN, HEAD, HEAD), BF),
        vmem((2, OWN, ROWS, HEAD), F32),
        vmem((OWN, HEAD + 16, HEAD), BF),
        vmem((QUAD, 2, HEAD + 16, HEAD), BF),
        vmem((QUAD, 80, HEAD), BF),
        vmem((QUAD, 80, HEAD), BF),
        vmem((QUAD, 64, HEAD), BF),
        vmem((QUAD, 64, HEAD), BF),
        vmem((QUAD, 2, HEAD, HEAD), BF),
        vmem((QUAD, 2, HEAD, HEAD), BF),
        vmem((Z, 128, HALF), BF),
        vmem((HEADS, 2 * ROWS, HEAD), BF),
        vmem((PARTS, 2 * ROWS, COLS), F32),
        vmem((2, PARTS, ROWS, COLS), BF),
        dma((8,)),
        dma((3,)), dma((3,)),
        dma((2, 8, SUBS)), dma((2, 8, SUBS)),
        *(dma((QUAD,)) for _ in range(8)),
        dma((OWN,)), dma((OWN,)),
        dma((2, PARTS)), dma((2, PARTS)),
    ]
    out = pl.pallas_call(
        kernel,
        out_shape=jax.ShapeDtypeStruct((ROWS, WIDTH), BF),
        in_specs=[pl.BlockSpec(memory_space=pltpu.HBM)] * 8,
        out_specs=pl.BlockSpec(memory_space=pltpu.HBM),
        scratch_shapes=scratch,
        compiler_params=pltpu.CompilerParams(
            collective_id=0, has_side_effects=True, vmem_limit_bytes=64 * 2**20 - 2**16
        ),
        name="retention_layer",
    )(
        x_in[0, 0], q_gain, key_gain_per_layer, out_gain, log_decay[0].T, out_weight[0], coarse, fine
    )
    return out[None, None]


def solution(mesh):
    placed = (
        P("pipe", None, "ctx", None),
        P("pipe", None),
        P("pipe", None),
        P("pipe", None),
        P("pipe", "ctx", None),
        P("pipe", "ctx", None),
    )
    return jax.shard_map(
        per_device,
        mesh=mesh,
        in_specs=placed,
        out_specs=P("pipe", None, "ctx", None),
        check_vma=False,
    )
```
